256 devices in a mesh: genome: 32 (over z, x), group: 8 (over y, core).
Axes of the slice: x: 4, y: 4, z: 8, core: 2. Of those that a mesh axis runs over, the one named last changes fastest.
Arguments:
- force: float32 [512, 32768], P('group', 'genome'), may hold values from -6 to 6
- pulled: int32 [512], P('group'), may hold values from 0 to 32767
- shift: float32 [32768], P('genome'), may hold values from 1 to 3
- bond: float32 [32768], P('genome'), may hold values from 0.25 to 1
- near_panel: bfloat16 [128, 256, 256], P('genome'), may hold values from -0.25 to 0.25
- far_panel: bfloat16 [128, 32, 256, 256], P('genome', 'group'), may hold values from -0.046875 to 0.046875
- far_index: int32 [128, 32], P('genome'), may hold values from 0 to 127, as said below
- far_count: int32 [128], P('genome'), may hold values from 1 to 32, as said below
Outputs:
- response: float32 [512, 32768], P('group', 'genome')
The draws below stay inside these ranges and needn't reach their ends.
Inputs may be any that keep to these rules, and one draw needn't show every extreme that they name: `far_count`: rows of one index of genome share a level of their own, so loads differ between devices; some row in every draw uses all 32 slots. far_index[r, s] // 4 differs from r // 4 by at most 16, and by exactly 16 for some slot in every draw.
All inputs are finite; a program needn't handle non-finite values.
Results may differ from the reference program's by a relative error of at most 0.0015.
Values may be sent and summed in bfloat16 or wider, within the bound.
No kernel may reach another device: no remote copies, remote signals or barrier semaphores. Data moves between devices by JAX's collectives and lax.ppermute only.
A program may use at most 128 MiB of HBM per device.

```python
import math
import jax
import jax.numpy as jnp
from jax import lax

BLK = 256
COLS = 512
FAR = 32
BLK_DEV = 4
BLOCKS = 128
BEADS = 32768
REACH_DEV = 16


def draw_far_count(key, part):
    key = jax.random.fold_in(key, 11)
    key_level, key_rows, key_pick = jax.random.split(key, 3)
    level = jax.random.randint(key_level, (BLOCKS // BLK_DEV, 1), 1, FAR + 1)
    raw_counts = jax.random.randint(key_rows, (BLOCKS // BLK_DEV, BLK_DEV), 0, FAR)
    counts = (1 + raw_counts % level).reshape(BLOCKS)
    chosen_row = jax.random.randint(key_pick, (), 0, BLOCKS)
    return jnp.where(jnp.arange(BLOCKS) == chosen_row, FAR, counts).astype(jnp.int32)


def draw_far_index(key, part):
    key = jax.random.fold_in(key, 23)
    key_offset, key_inner = jax.random.split(key, 2)
    runs = BLOCKS // BLK_DEV
    home = (jnp.arange(BLOCKS, dtype=jnp.int32) // BLK_DEV)[:, None]
    offset = jax.random.randint(key_offset, (BLOCKS, FAR), -REACH_DEV, REACH_DEV + 1)
    target = jnp.clip(home + offset, 0, runs - 1)
    first = lax_row_zero(BLOCKS, FAR) * (REACH_DEV - target)
    target = target + first
    inner = jax.random.randint(key_inner, (BLOCKS, FAR), 0, BLK_DEV)
    return (target * BLK_DEV + inner).astype(jnp.int32)


def lax_row_zero(rows, slots):
    row_ids = jnp.arange(rows, dtype=jnp.int32)[:, None]
    slot_ids = jnp.arange(slots, dtype=jnp.int32)[None, :]
    return ((row_ids == 0) & (slot_ids == 0)).astype(jnp.int32)


def plant(entries, stream_key, low, top_value):
    index_at = [jax.random.randint(jax.random.fold_in(stream_key, axis), (), 0, length) for axis, length in enumerate(entries.shape)]
    widest = entries.shape.index(max(entries.shape))
    neighbour = index_at[:widest] + [(index_at[widest] + 1) % entries.shape[widest]] + index_at[widest + 1:]
    return entries.at[tuple(index_at)].set(low).at[tuple(neighbour)].set(top_value)


def block_scale(stream_key, extent, cuts, low, top_value):
    def one(dim, parts):
        heights = jax.random.uniform(jax.random.fold_in(jax.random.fold_in(stream_key, 6), dim), (parts,), jnp.float32, low / len(cuts), top_value / len(cuts))
        return jnp.repeat(jnp.exp(heights), extent[dim] // parts).reshape((-1,) + (1,) * (len(extent) - dim - 1))

    loudness = one(*cuts[0])
    for cut in cuts[1:]:
        loudness = loudness * one(*cut)
    return loudness


def noise(rng, extent, spread, limit, shards=(), kind=jnp.bfloat16):
    drawn = jax.random.normal(rng, extent, jnp.float32) * spread
    if len(shards) > 0:
        drawn = block_scale(rng, extent, shards, -0.22, 0.18) * drawn
    return jnp.clip(drawn, min=-limit, max=limit).astype(kind)


def setup_inputs(seed: int = 0) -> dict:
    arg_keys = jax.random.split(jax.random.key(seed), 9)
    force = noise(arg_keys[0], (COLS, BEADS), 1.0, 6.0, ((0, 8), (1, 32)), jnp.float32)
    pulled = plant(jax.random.randint(arg_keys[1], (COLS,), 0, BEADS), jax.random.fold_in(arg_keys[1], 1), 0, BEADS - 1).astype(jnp.int32)
    shift = jnp.clip(1.0 + 2.0 * jax.random.uniform(arg_keys[2], (BEADS,), jnp.float32) ** block_scale(arg_keys[2], (BEADS,), ((0, 32),), -0.2, 0.2), 1.0, 3.0)
    bond = jnp.clip(jnp.exp(math.log(1.0) - 1.3862944 * jax.random.uniform(arg_keys[3], (BEADS,), jnp.float32) ** block_scale(arg_keys[3], (BEADS,), ((0, 32),), -0.2, 0.2)), 0.25, 1.0)
    near_panel = noise(arg_keys[4], (BLOCKS, BLK, BLK), (2 * BLK) ** -0.5, 0.25, ((0, 32),))
    far_panel = noise(arg_keys[5], (BLOCKS, FAR, BLK, BLK), (2 * BLK * FAR) ** -0.5, 0.046875, ((0, 32), (1, 8)))
    far_index = draw_far_index(jax.random.fold_in(arg_keys[8], 71), 0)
    far_count = draw_far_count(jax.random.fold_in(arg_keys[8], 71), 0)
    return dict(force=force, pulled=pulled, shift=shift, bond=bond, near_panel=near_panel, far_panel=far_panel, far_index=far_index, far_count=far_count)


CENTER = 4.0
HALF_WIDTH = 3.5
PULL_FORCE = 4.0

def cheb_coef():
    root_value = math.sqrt(CENTER * CENTER - HALF_WIDTH * HALF_WIDTH)
    ratio = (CENTER - root_value) / HALF_WIDTH
    return [1.0 / root_value] + [2.0 / root_value * (-ratio) ** k for k in range(1, 4)]

def reference(force, pulled, shift, bond, near_panel, far_panel, far_index, far_count):
    position = lax.broadcasted_iota(jnp.int32, (1, BEADS), 1)
    source = force + PULL_FORCE * (position == pulled[:, None]).astype(jnp.float32)
    link = jnp.where(position[0] < BEADS - 1, bond, jnp.float32(0.0))
    prior = jnp.concatenate([jnp.zeros((1,), jnp.float32), link[:-1]])
    diagonal = shift + link + prior
    slot_mask = (lax.broadcasted_iota(jnp.int32, (BLOCKS, FAR), 1) < far_count[:, None]).astype(jnp.bfloat16)

    def operate(field):
        rounded = field.astype(jnp.bfloat16)
        blocks = rounded.reshape(COLS, BLOCKS, BLK)
        near_term = jnp.einsum('crb,rba->cra', blocks.astype(jnp.float32), near_panel.astype(jnp.float32)).reshape(COLS, BEADS)

        def one_row(items):
            row_index, row_panel, row_mask = items
            chosen = blocks[:, row_index] * row_mask[None, :, None]
            return jnp.dot(chosen.reshape(COLS, FAR * BLK), row_panel.reshape(FAR * BLK, BLK), preferred_element_type=jnp.float32)
        far_rows = lax.map(one_row, (far_index, far_panel, slot_mask))
        far_term = jnp.transpose(far_rows, (1, 0, 2)).reshape(COLS, BEADS)
        padded = jnp.pad(field, ((0, 0), (1, 1)))
        chain = diagonal * field - link * padded[:, 2:] - prior * padded[:, :-2]
        return chain - near_term - far_term

    def scaled(field):
        return (operate(field) - CENTER * field) / HALF_WIDTH
    coef = cheb_coef()
    term_zero = source
    term_one = scaled(term_zero)
    term_two = 2.0 * scaled(term_one) - term_zero
    term_three = 2.0 * scaled(term_two) - term_one
    return coef[0] * term_zero + coef[1] * term_one + coef[2] * term_two + coef[3] * term_three
```

```python
import functools
import math

import jax
import jax.numpy as jnp
from jax import lax
from jax.experimental import pallas as pl
from jax.experimental.pallas import tpu as pltpu
from jax.sharding import PartitionSpec as P

CENTER = 4.0
HALF_WIDTH = 3.5
PULL_FORCE = 4.0

NZ, NX, NY, NC = 8, 4, 4, 2
BLK = 256
ROWS = 4
CHUNK = 4
COLS = 64
HALF = COLS // 2
BEADS = ROWS * BLK
VMEM_LIMIT = 44 * 1024 * 1024


def cheb_coef():
    root_value = math.sqrt(CENTER * CENTER - HALF_WIDTH * HALF_WIDTH)
    ratio = (CENTER - root_value) / HALF_WIDTH
    return [1.0 / root_value] + [2.0 / root_value * (-ratio) ** k for k in range(1, 4)]


def take_z(block, offset):
    route = [
        (((z + offset) % NZ) * NX + x, z * NX + x) for z in range(NZ) for x in range(NX)
    ]
    return lax.ppermute(block, "genome", route)


def take_x(block, offset):
    route = [
        (z * NX + (x + offset) % NX, z * NX + x) for z in range(NZ) for x in range(NX)
    ]
    return lax.ppermute(block, "genome", route)


def take_y(block, offset):
    route = [
        (((y + offset) % NY) * NC + c, y * NC + c) for y in range(NY) for c in range(NC)
    ]
    return lax.ppermute(block, "group", route)


def take_core(block):
    route = [(y * NC + 1 - c, y * NC + c) for y in range(NY) for c in range(NC)]
    return lax.ppermute(block, "group", route)


def ring(block, take, size):
    found = {0: block}
    for step in range(1, size // 2):
        found[step] = take(found[step - 1], 1)
        found[-step % size] = take(found[-(step - 1) % size], -1)
    mid = block.shape[0] // 2
    far = size // 2
    low = take(found[far - 1][:mid], 1)
    high = take(found[far + 1][mid:], -1)
    return [found[k] if k != far else (low, high) for k in range(size)]


def gathered(part_a, part_b):
    ax = ring(part_a, take_x, NX)
    ax[2] = jnp.concatenate(ax[2], axis=0)
    bz = ring(part_b, take_z, NZ)
    bz[4] = jnp.concatenate(bz[4], axis=0)
    az = ring(jnp.stack(ax), take_z, NZ)
    bx = ring(jnp.stack(bz), take_x, NX)
    flat_a = [*az[:4], *az[4], *az[5:]]
    flat_b = [*bx[:2], *bx[2], *bx[3:]]
    return flat_a, flat_b


def source_kernel(first_ref, pulled_ref, force_ref, source_ref, a_ref, b_ref):
    position = first_ref[0] + lax.broadcasted_iota(jnp.int32, (COLS, BEADS), 1)
    hit = position == pulled_ref[...]
    source = force_ref[...] + jnp.where(hit, jnp.float32(PULL_FORCE), jnp.float32(0.0))
    source_ref[...] = source
    put_rounded(source, a_ref, b_ref)


def put_rounded(field, a_ref, b_ref):
    rounded = field.astype(jnp.bfloat16)
    for r in range(ROWS):
        a_ref[r] = rounded[:HALF, r * BLK : (r + 1) * BLK]
        b_ref[r] = rounded[HALF:, r * BLK : (r + 1) * BLK]


def term_kernel(step, *refs):
    where_ref, index_ref, count_ref = refs[:3]
    refs = refs[3:]
    a_refs, refs = refs[: NZ + 1], refs[NZ + 1 :]
    b_refs, refs = refs[: NX + 1], refs[NX + 1 :]
    panel_refs, refs = refs[:10], refs[10:]
    near_ref, vec_ref = refs[:2]
    terms, refs = refs[2 : 2 + step], refs[2 + step :]
    if step < 3:
        out_ref, a_out, b_out = refs[:3]
        refs = refs[3:]
    else:
        out_ref = refs[0]
        refs = refs[1:]
    field, panels, total, field_sem, panel_sem = refs
    z, x, y, core = (where_ref[k] for k in range(4))

    copies = []
    for k, ref in enumerate(a_refs):
        if k == 4:
            dst = field.at[4, 0:2, :, 0:HALF, :]
        elif k == 5:
            dst = field.at[4, 2:4, :, 0:HALF, :]
        else:
            dst = field.at[k if k < 4 else k - 1, :, :, 0:HALF, :]
        copies.append(pltpu.make_async_copy(ref, dst, field_sem.at[k]))
    for k, ref in enumerate(b_refs):
        if k == 2:
            dst = field.at[0:4, 2, :, HALF:COLS, :]
        elif k == 3:
            dst = field.at[4:8, 2, :, HALF:COLS, :]
        else:
            dst = field.at[:, k if k < 2 else k - 1, :, HALF:COLS, :]
        copies.append(pltpu.make_async_copy(ref, dst, field_sem.at[NZ + 1 + k]))
    for copy in copies:
        copy.start()

    chunks = []
    for dc in range(NC):
        own = panel_refs[dc * 5 : dc * 5 + 5]
        for slot, dy in enumerate((0, 1, 3, 2)):
            j = ((y + dy) & (NY - 1)) * NC + ((core + dc) & 1)
            for r in range(ROWS):
                if dy == 2:
                    src = own[3 + r // 2].at[r % 2]
                else:
                    src = own[slot].at[r]
                n = (dc * 4 + slot) * ROWS + r
                copy = pltpu.make_async_copy(src, panels.at[n], panel_sem.at[n])
                chunks.append((slot, n, r, j, copy))
    chunks.sort(key=lambda c: (c[0], c[1]))
    for _, n, r, j, copy in chunks:
        pl.when(j * CHUNK < count_ref[r])(copy.start)
    for copy in copies:
        copy.wait()

    for r in range(ROWS):
        total[r] = jnp.dot(field[0, 0, r], near_ref[r], preferred_element_type=jnp.float32)

    def one(n, r, j, copy):
        @pl.when(j * CHUNK < count_ref[r])
        def _():
            copy.wait()
            acc = total[r]
            for k in range(CHUNK):
                s = j * CHUNK + k
                f = index_ref[r, s]
                dz = ((f >> 4) - z) & (NZ - 1)
                dx = ((f >> 2) - x) & (NX - 1)
                block = field[dz, dx, f & 3]
                block = jnp.where(s < count_ref[r], block, jnp.zeros_like(block))
                acc += jnp.dot(block, panels[n, k], preferred_element_type=jnp.float32)
            total[r] = acc

    for _, n, r, j, copy in chunks:
        one(n, r, j, copy)

    v = terms[0][...]
    left = field[jnp.where(x > 0, 0, NZ - 1), NX - 1, ROWS - 1][:, BLK - 128 :].astype(jnp.float32)
    right = field[jnp.where(x < NX - 1, 0, 1), 1, 0][:, :128].astype(jnp.float32)
    wide = jnp.concatenate([left, v, right], axis=1)
    width = BEADS + 256
    before = pltpu.roll(wide, 1, 1)[:, 128 : 128 + BEADS]
    after = pltpu.roll(wide, width - 1, 1)[:, 128 : 128 + BEADS]
    diagonal, link, prior = (vec_ref[k : k + 1, :] for k in range(3))
    chain = diagonal * v - link * after - prior * before
    contact = jnp.concatenate([total[r] for r in range(ROWS)], axis=1)
    scaled = (chain - contact - CENTER * v) / HALF_WIDTH
    coef = cheb_coef()
    if step == 1:
        new = scaled
    else:
        new = 2.0 * scaled - terms[1][...]
    if step < 3:
        out_ref[...] = new
        put_rounded(new, a_out, b_out)
    else:
        out_ref[...] = (
            coef[0] * terms[2][...] + coef[1] * terms[1][...] + coef[2] * v + coef[3] * new
        )


def term_call(step, where, index, count, parts, panels, near, vec, terms):
    flat_a, flat_b = parts
    smem = pl.BlockSpec(memory_space=pltpu.SMEM)
    vmem = pl.BlockSpec(memory_space=pltpu.VMEM)
    hbm = pl.BlockSpec(memory_space=pl.ANY)
    full = jax.ShapeDtypeStruct((COLS, BEADS), jnp.float32)
    half = jax.ShapeDtypeStruct((ROWS, HALF, BLK), jnp.bfloat16)
    moved = [*flat_a, *flat_b, *panels]
    return pl.pallas_call(
        functools.partial(term_kernel, step),
        out_shape=(full, half, half) if step < 3 else full,
        in_specs=[smem] * 3 + [hbm] * len(moved) + [vmem] * (2 + len(terms)),
        out_specs=(vmem,) * 3 if step < 3 else vmem,
        scratch_shapes=[
            pltpu.VMEM((NZ, NX, ROWS, COLS, BLK), jnp.bfloat16),
            pltpu.VMEM((8 * ROWS, CHUNK, BLK, BLK), jnp.bfloat16),
            pltpu.VMEM((ROWS, COLS, BLK), jnp.float32),
            pltpu.SemaphoreType.DMA((NZ + NX + 2,)),
            pltpu.SemaphoreType.DMA((8 * ROWS,)),
        ],
        compiler_params=pltpu.CompilerParams(vmem_limit_bytes=VMEM_LIMIT),
        cost_estimate=pl.CostEstimate(
            flops=2 * 128 * COLS * BLK * BLK, bytes_accessed=20 * 2**20, transcendentals=0
        ),
        name=f"term{step}",
    )(where, index, count, *moved, near, vec, *terms)


def per_device(force, pulled, shift, bond, near_panel, far_panel, far_index, far_count):
    genome, group = lax.axis_index("genome"), lax.axis_index("group")
    where = jnp.stack([genome // NX, genome % NX, group // NC, group % NC]).astype(jnp.int32)
    first_bead = (genome * BEADS).astype(jnp.int32)
    vmem = pl.BlockSpec(memory_space=pltpu.VMEM)
    half = jax.ShapeDtypeStruct((ROWS, HALF, BLK), jnp.bfloat16)
    source, part_a, part_b = pl.pallas_call(
        source_kernel,
        out_shape=(jax.ShapeDtypeStruct((COLS, BEADS), jnp.float32), half, half),
        in_specs=[pl.BlockSpec(memory_space=pltpu.SMEM), vmem, vmem],
        out_specs=(vmem,) * 3,
        name="source",
    )(first_bead[None], pulled[:, None], force)

    def split_ring(mine):
        found = ring(mine, take_y, NY)
        return [found[0], found[1], found[3], *found[2]]

    own = split_ring(far_panel)
    panels = own + [take_core(piece) for piece in own]

    position = first_bead + lax.iota(jnp.int32, BEADS)
    link = jnp.where(position < BEADS * NZ * NX - 1, bond, jnp.float32(0.0))
    left_bond = lax.ppermute(link[-1:], "genome", [(g, g + 1) for g in range(NZ * NX - 1)])
    prior = jnp.concatenate([left_bond, link[:-1]])
    vec = jnp.stack([shift + link + prior, link, prior])

    call = functools.partial(term_call)
    parts = gathered(part_a, part_b)
    one, part_a, part_b = call(1, where, far_index, far_count, parts, panels, near_panel, vec, [source])
    parts = gathered(part_a, part_b)
    two, part_a, part_b = call(2, where, far_index, far_count, parts, panels, near_panel, vec, [one, source])
    parts = gathered(part_a, part_b)
    return call(3, where, far_index, far_count, parts, panels, near_panel, vec, [two, one, source])


def solution(mesh):
    in_specs = (
        P("group", "genome"),
        P("group"),
        P("genome"),
        P("genome"),
        P("genome", None, None),
        P("genome", "group", None, None),
        P("genome", None),
        P("genome"),
    )
    out_specs = P("group", "genome")
    return jax.shard_map(
        per_device, mesh=mesh, in_specs=in_specs, out_specs=out_specs, check_vma=False
    )
```

```python
import functools
import math

import jax
import jax.numpy as jnp
from jax import lax
from jax.experimental import pallas as pl
from jax.experimental.pallas import tpu as pltpu
from jax.sharding import PartitionSpec as P

CENTER = 4.0
HALF_WIDTH = 3.5
PULL_FORCE = 4.0

NZ, NX, NY, NC = 8, 4, 4, 2
BLK = 256
ROWS = 4
CHUNK = 4
COLS = 64
PANELS = 14
BEADS = ROWS * BLK
VMEM_LIMIT = 26 * 1024 * 1024


def cheb_coef():
    root_value = math.sqrt(CENTER * CENTER - HALF_WIDTH * HALF_WIDTH)
    ratio = (CENTER - root_value) / HALF_WIDTH
    return [1.0 / root_value] + [2.0 / root_value * (-ratio) ** k for k in range(1, 4)]


def partner(x, kind):
    return x ^ 1 if kind == 0 else (((x - 1) ^ 1) + 1) % NX


def take_z(block, offset):
    route = [
        (((z + offset) % NZ) * NX + x, z * NX + x) for z in range(NZ) for x in range(NX)
    ]
    return lax.ppermute(block, "genome", route)


def take_pair(block, flip):
    route = []
    for g in range(NZ * NX):
        for j in range(NY * NC):
            src = g - g % NX + partner(g % NX, (j % NC) ^ flip)
            route.append((src * NY * NC + j, g * NY * NC + j))
    return lax.ppermute(block, ("genome", "group"), route)


def take_y(block, offset):
    route = [
        (((y + offset) % NY) * NC + c, y * NC + c) for y in range(NY) for c in range(NC)
    ]
    return lax.ppermute(block, "group", route)


def take_core(block):
    route = [(y * NC + 1 - c, y * NC + c) for y in range(NY) for c in range(NC)]
    return lax.ppermute(block, "group", route)


def gathered(own):
    pair = jnp.stack([own, take_pair(own, 0)])
    up, down = take_z(pair, 1), take_z(pair, -1)
    near = jnp.concatenate([pair, up, down])
    near_other = take_pair(near, 1)
    up, down = take_z(up, 1), take_z(down, -1)
    mid = jnp.concatenate([up, down])
    mid_other = take_pair(mid, 1)
    up, down = take_z(up, 1), take_z(down, -1)
    wide = jnp.concatenate([up, down])
    wide_other = take_pair(wide, 1)
    up, down = take_z(up[:1], 1), take_z(down[1:], -1)
    last = jnp.concatenate([up, down])
    last_other = take_pair(last, 1)
    return [near, mid, wide, last, near_other, mid_other, wide_other, last_other]


def pair_tables():
    by_z = {0: 0, 1: 2, 7: 4, 2: 6, 6: 8, 3: 10, 5: 12, 4: 14}
    out = []
    for core in range(NC):
        for x in range(NX):
            other = partner(x, core ^ 1)
            place = {x: 0, partner(x, core): 1, other: 16, partner(other, core): 17}
            out.append(
                [by_z[dz] + place[(x + dx) % NX] for dz in range(NZ) for dx in range(NX)]
            )
    return out


def source_kernel(first_ref, pulled_ref, force_ref, source_ref, own_ref):
    position = first_ref[0] + lax.broadcasted_iota(jnp.int32, (COLS, BEADS), 1)
    here = lax.broadcasted_iota(jnp.int32, (COLS, COLS), 0)
    there = lax.broadcasted_iota(jnp.int32, (COLS, COLS), 1)
    chosen = jnp.where(here == there, pulled_ref[...].astype(jnp.float32), jnp.float32(0.0))
    hit = position == jnp.sum(chosen, axis=1, keepdims=True).astype(jnp.int32)
    source = force_ref[...] + jnp.where(hit, jnp.float32(PULL_FORCE), jnp.float32(0.0))
    source_ref[...] = source
    put_rounded(source, own_ref)


def put_rounded(field, own_ref):
    rounded = field.astype(jnp.bfloat16)
    for r in range(ROWS):
        own_ref[r] = rounded[:, r * BLK : (r + 1) * BLK]


def term_kernel(step, *refs):
    where_ref, table_ref, index_ref, count_ref = refs[:4]
    refs = refs[4:]
    count = 1 if step == 1 else 8
    piece_refs, refs = refs[:count], refs[count:]
    panel_refs, refs = refs[:PANELS], refs[PANELS:]
    near_hbm, vec_ref = refs[:2]
    terms, refs = refs[2 : 2 + step], refs[2 + step :]
    if step < 3:
        out_ref, own_out = refs[:2]
        refs = refs[2:]
    else:
        out_ref = refs[0]
        refs = refs[1:]
    field, panels, near_ref, total, field_sem, panel_sem = refs
    z, x, y, core = (where_ref[k] for k in range(4))

    copies, at = [], 0
    for k, ref in enumerate(piece_refs):
        dst = field.at[at : at + ref.shape[0]]
        copies.append(pltpu.make_async_copy(ref, dst, field_sem.at[k]))
        at += ref.shape[0]
    copies.append(pltpu.make_async_copy(near_hbm, near_ref, field_sem.at[8]))
    for copy in copies:
        copy.start()

    def slots_of(n):
        dc, slot = n >> 4, (n >> 2) & 3
        dy = slot ^ (slot >> 1)
        return (((y + dy) & (NY - 1)) * NC + ((core + dc) & 1)) * CHUNK

    for n in range(8 * ROWS):
        dc, slot, r = n // 16, (n // ROWS) % NY, n % ROWS
        ref = panel_refs[dc * 7 + (0 if slot == 0 else 2 * slot - 1 + r // 2)]
        src = ref.at[r if slot == 0 else r % 2]
        copy = pltpu.make_async_copy(src, panels.at[n], panel_sem.at[n])
        pl.when(slots_of(n) < count_ref[r])(copy.start)
    for copy in copies:
        copy.wait()

    for r in range(ROWS):
        total[r] = jnp.dot(field[table_ref[0], r], near_ref[r], preferred_element_type=jnp.float32)

    @pl.loop(0, 8 * ROWS)
    def _(n):
        r, first = n & (ROWS - 1), slots_of(n)

        @pl.when(first < count_ref[r])
        def _():
            pltpu.make_async_copy(panels.at[n], panels.at[n], panel_sem.at[n]).wait()
            acc = total[r]
            for k in range(CHUNK):
                f = index_ref[r, first + k]
                dz = ((f >> 4) - z) & (NZ - 1)
                dx = ((f >> 2) - x) & (NX - 1)
                block = field[table_ref[dz * NX + dx], f & 3]
                block = jnp.where(first + k < count_ref[r], block, jnp.zeros_like(block))
                acc += jnp.dot(block, panels[n, k], preferred_element_type=jnp.float32)
            total[r] = acc

    v = terms[0][...]
    left_at = table_ref[jnp.where(x > 0, 0, NZ - 1) * NX + NX - 1]
    right_at = table_ref[jnp.where(x < NX - 1, 0, 1) * NX + 1]
    left = field[left_at, ROWS - 1][:, BLK - 128 :].astype(jnp.float32)
    right = field[right_at, 0][:, :128].astype(jnp.float32)
    wide = jnp.concatenate([left, v, right], axis=1)
    width = BEADS + 256
    before = pltpu.roll(wide, 1, 1)[:, 128 : 128 + BEADS]
    after = pltpu.roll(wide, width - 1, 1)[:, 128 : 128 + BEADS]
    diagonal, link, prior = (vec_ref[k : k + 1, :] for k in range(3))
    chain = diagonal * v - link * after - prior * before
    contact = jnp.concatenate([total[r] for r in range(ROWS)], axis=1)
    scaled = (chain - contact - CENTER * v) / HALF_WIDTH
    coef = cheb_coef()
    if step == 1:
        new = scaled
    else:
        new = 2.0 * scaled - terms[1][...]
    if step < 3:
        out_ref[...] = new
        put_rounded(new, own_out)
    else:
        out_ref[...] = (
            coef[0] * terms[2][...] + coef[1] * terms[1][...] + coef[2] * v + coef[3] * new
        )


def term_call(step, scalars, pieces, panels, near, vec, terms):
    kept = pltpu.VMEM if step > 1 else pltpu.HBM
    pieces = [pltpu.with_memory_space_constraint(p, kept) for p in pieces]
    panels = [pltpu.with_memory_space_constraint(p, pltpu.HBM) for p in panels]
    near = pltpu.with_memory_space_constraint(near, pltpu.HBM)
    smem = pl.BlockSpec(memory_space=pltpu.SMEM)
    vmem = pl.BlockSpec(memory_space=pltpu.VMEM)
    hbm = pl.BlockSpec(memory_space=pltpu.HBM)
    resident = pl.BlockSpec(memory_space=kept)
    full = jax.ShapeDtypeStruct((COLS, BEADS), jnp.float32)
    own = jax.ShapeDtypeStruct((ROWS, COLS, BLK), jnp.bfloat16)
    return pl.pallas_call(
        functools.partial(term_kernel, step),
        out_shape=(full, own) if step < 3 else full,
        in_specs=[smem] * 4 + [resident] * len(pieces) + [hbm] * PANELS + [hbm] + [vmem] * (1 + len(terms)),
        out_specs=(vmem,) * 2 if step < 3 else vmem,
        scratch_shapes=[
            pltpu.VMEM((NZ * NX, ROWS, COLS, BLK), jnp.bfloat16),
            pltpu.VMEM((8 * ROWS, CHUNK, BLK, BLK), jnp.bfloat16),
            pltpu.VMEM((ROWS, BLK, BLK), jnp.bfloat16),
            pltpu.VMEM((ROWS, COLS, BLK), jnp.float32),
            pltpu.SemaphoreType.DMA((9,)),
            pltpu.SemaphoreType.DMA((8 * ROWS,)),
        ],
        compiler_params=pltpu.CompilerParams(vmem_limit_bytes=VMEM_LIMIT),
        cost_estimate=pl.CostEstimate(
            flops=2 * 128 * COLS * BLK * BLK, bytes_accessed=20 * 2**20, transcendentals=0
        ),
        name=f"term{step}",
    )(*scalars, *pieces, *panels, near, vec, *terms)


def ring_of_panels(own):
    low, high = own[:2], own[2:]
    up_low = take_y(low, 1)
    down_high = take_y(high, -1)
    up_high = take_y(high, 1)
    down_low = take_y(low, -1)
    far_low = take_y(up_low, 1)
    far_high = take_y(down_high, -1)
    return [own, up_low, up_high, down_low, down_high, far_low, far_high]


def per_device(force, pulled, shift, bond, near_panel, far_panel, far_index, far_count):
    genome, group = lax.axis_index("genome"), lax.axis_index("group")
    core = group % NC
    where = jnp.stack([genome // NX, genome % NX, group // NC, core]).astype(jnp.int32)
    offset = lax.iota(jnp.int32, NZ * NX)
    by_place = (where[0] * NX + (offset // NX) * NX) % (NZ * NX) + (where[1] + offset % NX) % NX
    by_pair = jnp.array(pair_tables(), jnp.int32)[core * NX + where[1]]
    first_bead = (genome * BEADS).astype(jnp.int32)

    found = ring_of_panels(far_panel)
    panels = found + [take_core(piece) for piece in found]

    vmem = pl.BlockSpec(memory_space=pltpu.VMEM)
    source, own = pl.pallas_call(
        source_kernel,
        out_shape=(
            jax.ShapeDtypeStruct((COLS, BEADS), jnp.float32),
            jax.ShapeDtypeStruct((ROWS, COLS, BLK), jnp.bfloat16),
        ),
        in_specs=[pl.BlockSpec(memory_space=pltpu.SMEM), vmem, vmem],
        out_specs=(vmem,) * 2,
        name="source",
    )(first_bead[None], pulled[None, :], force)

    position = first_bead + lax.iota(jnp.int32, BEADS)
    link = jnp.where(position < BEADS * NZ * NX - 1, bond, jnp.float32(0.0))
    left_bond = lax.ppermute(link[-1:], "genome", [(g, g + 1) for g in range(NZ * NX - 1)])
    prior = jnp.concatenate([left_bond, link[:-1]])
    vec = jnp.stack([shift + link + prior, link, prior])

    everyone = lax.all_gather(own, "genome")
    scalars = (where, by_place, far_index, far_count)
    one, own = term_call(1, scalars, [everyone], panels, near_panel, vec, [source])
    scalars = (where, by_pair, far_index, far_count)
    two, own = term_call(2, scalars, gathered(own), panels, near_panel, vec, [one, source])
    return term_call(3, scalars, gathered(own), panels, near_panel, vec, [two, one, source])


def solution(mesh):
    in_specs = (
        P("group", "genome"),
        P("group"),
        P("genome"),
        P("genome"),
        P("genome", None, None),
        P("genome", "group", None, None),
        P("genome", None),
        P("genome"),
    )
    out_specs = P("group", "genome")
    return jax.shard_map(
        per_device, mesh=mesh, in_specs=in_specs, out_specs=out_specs, check_vma=False
    )
```

```python
import functools
import math

import jax
import jax.numpy as jnp
from jax import lax
from jax.experimental import pallas as pl
from jax.experimental.pallas import tpu as pltpu
from jax.sharding import PartitionSpec as P

CENTER = 4.0
HALF_WIDTH = 3.5
PULL_FORCE = 4.0

NZ, NX, NY, NC = 8, 4, 4, 2
BLK = 256
ROWS = 4
CHUNK = 4
COLS = 64
PANELS = 14
GROUPS = 10
LOOKAHEAD = 4
BEADS = ROWS * BLK
VMEM_LIMIT = 26 * 1024 * 1024


def cheb_coef():
    root_value = math.sqrt(CENTER * CENTER - HALF_WIDTH * HALF_WIDTH)
    ratio = (CENTER - root_value) / HALF_WIDTH
    return [1.0 / root_value] + [2.0 / root_value * (-ratio) ** k for k in range(1, 4)]


def partner(x, kind):
    return x ^ 1 if kind == 0 else (((x - 1) ^ 1) + 1) % NX


def take_z(block, offset):
    route = [
        (((z + offset) % NZ) * NX + x, z * NX + x) for z in range(NZ) for x in range(NX)
    ]
    return lax.ppermute(block, "genome", route)


def take_pair(block, flip):
    route = []
    for g in range(NZ * NX):
        for j in range(NY * NC):
            src = g - g % NX + partner(g % NX, (j % NC) ^ flip)
            route.append((src * NY * NC + j, g * NY * NC + j))
    return lax.ppermute(block, ("genome", "group"), route)


def take_y(block, offset):
    route = [
        (((y + offset) % NY) * NC + c, y * NC + c) for y in range(NY) for c in range(NC)
    ]
    return lax.ppermute(block, "group", route)


def take_core(block):
    route = [(y * NC + 1 - c, y * NC + c) for y in range(NY) for c in range(NC)]
    return lax.ppermute(block, "group", route)


def gathered(own):
    pair = jnp.stack([own, take_pair(own, 0)])
    up, down = take_z(pair, 1), take_z(pair, -1)
    pair_other = take_pair(pair, 1)
    near = jnp.concatenate([up, down])
    near_other = take_pair(near, 1)
    up, down = take_z(up, 1), take_z(down, -1)
    mid = jnp.concatenate([up, down])
    mid_other = take_pair(mid, 1)
    up, down = take_z(up, 1), take_z(down, -1)
    wide = jnp.concatenate([up, down])
    wide_other = take_pair(wide, 1)
    up, down = take_z(up[:1], 1), take_z(down[1:], -1)
    last = jnp.concatenate([up, down])
    last_other = take_pair(last, 1)
    return [pair, near, mid, wide, last, pair_other, near_other, mid_other, wide_other, last_other]


def pair_tables():
    by_z = {0: 0, 1: 2, 7: 4, 2: 6, 6: 8, 3: 10, 5: 12, 4: 14}
    out = []
    for core in range(NC):
        for x in range(NX):
            other = partner(x, core ^ 1)
            place = {x: 0, partner(x, core): 1, other: 16, partner(other, core): 17}
            out.append(
                [by_z[dz] + place[(x + dx) % NX] for dz in range(NZ) for dx in range(NX)]
            )
    return out


def source_kernel(first_ref, pulled_ref, force_ref, source_ref, own_ref):
    position = first_ref[0] + lax.broadcasted_iota(jnp.int32, (COLS, BEADS), 1)
    here = lax.broadcasted_iota(jnp.int32, (COLS, COLS), 0)
    there = lax.broadcasted_iota(jnp.int32, (COLS, COLS), 1)
    chosen = jnp.where(here == there, pulled_ref[...].astype(jnp.float32), jnp.float32(0.0))
    hit = position == jnp.sum(chosen, axis=1, keepdims=True).astype(jnp.int32)
    source = force_ref[...] + jnp.where(hit, jnp.float32(PULL_FORCE), jnp.float32(0.0))
    source_ref[...] = source
    put_rounded(source, own_ref)


def put_rounded(field, own_ref):
    rounded = field.astype(jnp.bfloat16)
    for r in range(ROWS):
        own_ref[r] = rounded[:, r * BLK : (r + 1) * BLK]


def put_piece(field, at, ref, k):
    field[at + k] = ref[k]


def term_kernel(step, *refs):
    where_ref, table_ref, index_ref, count_ref = refs[:4]
    refs = refs[4:]
    count = 1 if step == 1 else GROUPS
    piece_refs, refs = refs[:count], refs[count:]
    panel_refs, refs = refs[:PANELS], refs[PANELS:]
    near_hbm, vec_ref = refs[:2]
    terms, refs = refs[2 : 2 + step], refs[2 + step :]
    if step < 3:
        out_ref, own_out = refs[:2]
        refs = refs[2:]
    else:
        out_ref = refs[0]
        refs = refs[1:]
    field, panels, near_ref, total, field_sem, panel_sem = refs
    z, x, y, core = (where_ref[k] for k in range(4))

    copies = [pltpu.make_async_copy(near_hbm, near_ref, field_sem.at[1])]
    if step == 1:
        copies.append(pltpu.make_async_copy(piece_refs[0], field, field_sem.at[0]))
    for copy in copies:
        copy.start()

    def slots_of(n):
        dc, slot = n >> 4, (n >> 2) & 3
        dy = slot ^ (slot >> 1)
        return (((y + dy) & (NY - 1)) * NC + ((core + dc) & 1)) * CHUNK

    def rows_of(k):
        slot = (k % 7 + 1) // 2
        low = 0 if slot == 0 or k % 7 % 2 else 2
        return (k // 7 * NY + slot) * ROWS + low, panel_refs[k].shape[0]

    def fetch(k):
        at, rows = rows_of(k)
        for i in range(rows):
            copy = pltpu.make_async_copy(panel_refs[k].at[i], panels.at[at + i], panel_sem.at[at + i])
            pl.when(slots_of(at + i) < count_ref[(at + i) % ROWS])(copy.start)

    for k in range(LOOKAHEAD):
        fetch(k)
    at = 0
    for ref in piece_refs if step > 1 else ():
        pl.loop(0, ref.shape[0])(functools.partial(put_piece, field, at, ref))
        at += ref.shape[0]
    for copy in copies:
        copy.wait()

    for r in range(ROWS):
        total[r] = jnp.dot(field[table_ref[0], r], near_ref[r], preferred_element_type=jnp.float32)

    def contact(n):
        r, first = n & (ROWS - 1), slots_of(n)

        @pl.when(first < count_ref[r])
        def _():
            pltpu.make_async_copy(panels.at[n], panels.at[n], panel_sem.at[n]).wait()
            blocks = []
            for k in range(CHUNK):
                f = index_ref[r, first + k]
                dz = ((f >> 4) - z) & (NZ - 1)
                dx = ((f >> 2) - x) & (NX - 1)
                block = field[table_ref[dz * NX + dx], f & 3]
                blocks.append(jnp.where(first + k < count_ref[r], block, jnp.zeros_like(block)))
            total[r] += jnp.dot(
                jnp.concatenate(blocks, axis=1),
                panels[n].reshape(CHUNK * BLK, BLK),
                preferred_element_type=jnp.float32,
            )

    for k in range(PANELS):
        if k + LOOKAHEAD < PANELS:
            fetch(k + LOOKAHEAD)
        at, rows = rows_of(k)
        pl.loop(at, at + rows)(contact)

    v = terms[0][...]
    left_at = table_ref[jnp.where(x > 0, 0, NZ - 1) * NX + NX - 1]
    right_at = table_ref[jnp.where(x < NX - 1, 0, 1) * NX + 1]
    left = field[left_at, ROWS - 1][:, BLK - 128 :].astype(jnp.float32)
    right = field[right_at, 0][:, :128].astype(jnp.float32)
    wide = jnp.concatenate([left, v, right], axis=1)
    width = BEADS + 256
    before = pltpu.roll(wide, 1, 1)[:, 128 : 128 + BEADS]
    after = pltpu.roll(wide, width - 1, 1)[:, 128 : 128 + BEADS]
    diagonal, link, prior = (vec_ref[k : k + 1, :] for k in range(3))
    chain = diagonal * v - link * after - prior * before
    contact = jnp.concatenate([total[r] for r in range(ROWS)], axis=1)
    scaled = (chain - contact - CENTER * v) / HALF_WIDTH
    coef = cheb_coef()
    if step == 1:
        new = scaled
    else:
        new = 2.0 * scaled - terms[1][...]
    if step < 3:
        out_ref[...] = new
        put_rounded(new, own_out)
    else:
        out_ref[...] = (
            coef[0] * terms[2][...] + coef[1] * terms[1][...] + coef[2] * v + coef[3] * new
        )


def term_call(step, scalars, pieces, panels, near, vec, terms):
    kept = pltpu.VMEM if step > 1 else pltpu.HBM
    pieces = [pltpu.with_memory_space_constraint(p, kept) for p in pieces]
    panels = [pltpu.with_memory_space_constraint(p, pltpu.HBM) for p in panels]
    near = pltpu.with_memory_space_constraint(near, pltpu.HBM)
    smem = pl.BlockSpec(memory_space=pltpu.SMEM)
    vmem = pl.BlockSpec(memory_space=pltpu.VMEM)
    hbm = pl.BlockSpec(memory_space=pltpu.HBM)
    resident = vmem if step > 1 else hbm
    full = jax.ShapeDtypeStruct((COLS, BEADS), jnp.float32)
    own = jax.ShapeDtypeStruct((ROWS, COLS, BLK), jnp.bfloat16)
    return pl.pallas_call(
        functools.partial(term_kernel, step),
        out_shape=(full, own) if step < 3 else full,
        in_specs=[smem] * 4 + [resident] * len(pieces) + [hbm] * PANELS + [hbm] + [vmem] * (1 + len(terms)),
        out_specs=(vmem,) * 2 if step < 3 else vmem,
        scratch_shapes=[
            pltpu.VMEM((NZ * NX, ROWS, COLS, BLK), jnp.bfloat16),
            pltpu.VMEM((8 * ROWS, CHUNK, BLK, BLK), jnp.bfloat16),
            pltpu.VMEM((ROWS, BLK, BLK), jnp.bfloat16),
            pltpu.VMEM((ROWS, COLS, BLK), jnp.float32),
            pltpu.SemaphoreType.DMA((2,)),
            pltpu.SemaphoreType.DMA((8 * ROWS,)),
        ],
        compiler_params=pltpu.CompilerParams(vmem_limit_bytes=VMEM_LIMIT),
        cost_estimate=pl.CostEstimate(
            flops=2 * 128 * COLS * BLK * BLK, bytes_accessed=20 * 2**20, transcendentals=0
        ),
        name=f"term{step}",
    )(*scalars, *pieces, *panels, near, vec, *terms)


def ring_of_panels(own):
    low, high = own[:2], own[2:]
    up_low = take_y(low, 1)
    down_high = take_y(high, -1)
    up_high = take_y(high, 1)
    down_low = take_y(low, -1)
    far_low = take_y(up_low, 1)
    far_high = take_y(down_high, -1)
    return [own, up_low, up_high, down_low, down_high, far_low, far_high]


def per_device(force, pulled, shift, bond, near_panel, far_panel, far_index, far_count):
    genome, group = lax.axis_index("genome"), lax.axis_index("group")
    core = group % NC
    where = jnp.stack([genome // NX, genome % NX, group // NC, core]).astype(jnp.int32)
    offset = lax.iota(jnp.int32, NZ * NX)
    by_place = (where[0] * NX + (offset // NX) * NX) % (NZ * NX) + (where[1] + offset % NX) % NX
    by_pair = jnp.array(pair_tables(), jnp.int32)[core * NX + where[1]]
    first_bead = (genome * BEADS).astype(jnp.int32)

    found = ring_of_panels(far_panel)
    panels = found + [take_core(piece) for piece in found]

    vmem = pl.BlockSpec(memory_space=pltpu.VMEM)
    source, own = pl.pallas_call(
        source_kernel,
        out_shape=(
            jax.ShapeDtypeStruct((COLS, BEADS), jnp.float32),
            jax.ShapeDtypeStruct((ROWS, COLS, BLK), jnp.bfloat16),
        ),
        in_specs=[pl.BlockSpec(memory_space=pltpu.SMEM), vmem, vmem],
        out_specs=(vmem,) * 2,
        name="source",
    )(first_bead[None], pulled[None, :], force)

    position = first_bead + lax.iota(jnp.int32, BEADS)
    link = jnp.where(position < BEADS * NZ * NX - 1, bond, jnp.float32(0.0))
    left_bond = lax.ppermute(link[-1:], "genome", [(g, g + 1) for g in range(NZ * NX - 1)])
    prior = jnp.concatenate([left_bond, link[:-1]])
    vec = jnp.stack([shift + link + prior, link, prior])

    everyone = lax.all_gather(own, "genome")
    scalars = (where, by_place, far_index, far_count)
    one, own = term_call(1, scalars, [everyone], panels, near_panel, vec, [source])
    scalars = (where, by_pair, far_index, far_count)
    two, own = term_call(2, scalars, gathered(own), panels, near_panel, vec, [one, source])
    return term_call(3, scalars, gathered(own), panels, near_panel, vec, [two, one, source])


def solution(mesh):
    in_specs = (
        P("group", "genome"),
        P("group"),
        P("genome"),
        P("genome"),
        P("genome", None, None),
        P("genome", "group", None, None),
        P("genome", None),
        P("genome"),
    )
    out_specs = P("group", "genome")
    return jax.shard_map(
        per_device, mesh=mesh, in_specs=in_specs, out_specs=out_specs, check_vma=False
    )
```

```python
import functools
import math

import jax
import jax.numpy as jnp
from jax import lax
from jax.experimental import pallas as pl
from jax.experimental.pallas import tpu as pltpu
from jax.sharding import PartitionSpec as P

CENTER = 4.0
HALF_WIDTH = 3.5
PULL_FORCE = 4.0

NZ, NX, NY, NC = 8, 4, 4, 2
BLK = 256
ROWS = 4
CHUNK = 4
COLS = 64
PANELS = 14
GROUPS = 10
LOOKAHEAD = 4
BEADS = ROWS * BLK
VMEM_LIMIT = 26 * 1024 * 1024


def cheb_coef():
    root_value = math.sqrt(CENTER * CENTER - HALF_WIDTH * HALF_WIDTH)
    ratio = (CENTER - root_value) / HALF_WIDTH
    return [1.0 / root_value] + [2.0 / root_value * (-ratio) ** k for k in range(1, 4)]


def partner(x, kind):
    return x ^ 1 if kind == 0 else (((x - 1) ^ 1) + 1) % NX


def take_z(block, offset):
    route = [
        (((z + offset) % NZ) * NX + x, z * NX + x) for z in range(NZ) for x in range(NX)
    ]
    return lax.ppermute(block, "genome", route)


def take_pair(block, flip):
    route = []
    for g in range(NZ * NX):
        for j in range(NY * NC):
            src = g - g % NX + partner(g % NX, (j % NC) ^ flip)
            route.append((src * NY * NC + j, g * NY * NC + j))
    return lax.ppermute(block, ("genome", "group"), route)


def take_y(block, offset):
    route = [
        (((y + offset) % NY) * NC + c, y * NC + c) for y in range(NY) for c in range(NC)
    ]
    return lax.ppermute(block, "group", route)


def take_core(block):
    route = [(y * NC + 1 - c, y * NC + c) for y in range(NY) for c in range(NC)]
    return lax.ppermute(block, "group", route)


def gathered(own):
    pair = jnp.stack([own, take_pair(own, 0)])
    up, down = take_z(pair, 1), take_z(pair, -1)
    pair_other = take_pair(pair, 1)
    near = jnp.concatenate([up, down])
    near_other = take_pair(near, 1)
    up, down = take_z(up, 1), take_z(down, -1)
    mid = jnp.concatenate([up, down])
    mid_other = take_pair(mid, 1)
    up, down = take_z(up, 1), take_z(down, -1)
    wide = jnp.concatenate([up, down])
    wide_other = take_pair(wide, 1)
    up, down = take_z(up[:1], 1), take_z(down[1:], -1)
    last = jnp.concatenate([up, down])
    last_other = take_pair(last, 1)
    return [pair, near, mid, wide, last, pair_other, near_other, mid_other, wide_other, last_other]


def pair_tables():
    by_z = {0: 0, 1: 2, 7: 4, 2: 6, 6: 8, 3: 10, 5: 12, 4: 14}
    out = []
    for core in range(NC):
        for x in range(NX):
            other = partner(x, core ^ 1)
            place = {x: 0, partner(x, core): 1, other: 16, partner(other, core): 17}
            out.append(
                [by_z[dz] + place[(x + dx) % NX] for dz in range(NZ) for dx in range(NX)]
            )
    return out


def source_kernel(first_ref, pulled_ref, force_ref, source_ref, own_ref):
    position = first_ref[0] + lax.broadcasted_iota(jnp.int32, (COLS, BEADS), 1)
    here = lax.broadcasted_iota(jnp.int32, (COLS, COLS), 0)
    there = lax.broadcasted_iota(jnp.int32, (COLS, COLS), 1)
    chosen = jnp.where(here == there, pulled_ref[...].astype(jnp.float32), jnp.float32(0.0))
    hit = position == jnp.sum(chosen, axis=1, keepdims=True).astype(jnp.int32)
    source = force_ref[...] + jnp.where(hit, jnp.float32(PULL_FORCE), jnp.float32(0.0))
    source_ref[...] = source
    put_rounded(source, own_ref)


def put_rounded(field, own_ref):
    rounded = field.astype(jnp.bfloat16)
    for r in range(ROWS):
        own_ref[r] = rounded[:, r * BLK : (r + 1) * BLK]


def put_piece(field, at, ref, k):
    field[at + k] = ref[k]


def term_kernel(step, *refs):
    where_ref, table_ref, index_ref, count_ref = refs[:4]
    refs = refs[4:]
    count = 1 if step == 1 else GROUPS
    piece_refs, refs = refs[:count], refs[count:]
    panel_refs, refs = refs[:PANELS], refs[PANELS:]
    near_hbm, vec_ref = refs[:2]
    terms, refs = refs[2 : 2 + step], refs[2 + step :]
    if step < 3:
        out_ref, own_out = refs[:2]
        refs = refs[2:]
    else:
        out_ref = refs[0]
        refs = refs[1:]
    field, panels, near_ref, total, field_sem, panel_sem = refs
    z, x, y, core = (where_ref[k] for k in range(4))

    copies = [pltpu.make_async_copy(near_hbm, near_ref, field_sem.at[1])]
    if step == 1:
        copies.append(pltpu.make_async_copy(piece_refs[0], field, field_sem.at[0]))
    for copy in copies:
        copy.start()

    def slots_of(n):
        dc, slot = n >> 4, (n >> 2) & 3
        dy = slot ^ (slot >> 1)
        return (((y + dy) & (NY - 1)) * NC + ((core + dc) & 1)) * CHUNK

    def rows_of(k):
        slot = (k % 7 + 1) // 2
        low = 0 if slot == 0 or k % 7 % 2 else 2
        return (k // 7 * NY + slot) * ROWS + low, panel_refs[k].shape[0]

    def fetch(k):
        at, rows = rows_of(k)
        for i in range(rows):
            for m in range(CHUNK):
                copy = pltpu.make_async_copy(
                    panel_refs[k].at[i, m], panels.at[at + i, m], panel_sem.at[at + i, m]
                )
                pl.when(slots_of(at + i) + m < count_ref[(at + i) % ROWS])(copy.start)

    for k in range(LOOKAHEAD):
        fetch(k)
    at = 0
    for ref in piece_refs if step > 1 else ():
        pl.loop(0, ref.shape[0])(functools.partial(put_piece, field, at, ref))
        at += ref.shape[0]
    for copy in copies:
        copy.wait()

    for r in range(ROWS):
        total[r] = jnp.dot(field[table_ref[0], r], near_ref[r], preferred_element_type=jnp.float32)

    def contact(n):
        r, first = n & (ROWS - 1), slots_of(n)

        @pl.when(first < count_ref[r])
        def _():
            blocks, sources = [], []
            for k in range(CHUNK):
                copy = pltpu.make_async_copy(panels.at[n, k], panels.at[n, k], panel_sem.at[n, k])
                pl.when(first + k < count_ref[r])(copy.wait)
                panel = panels[n, k]
                sources.append(jnp.where(first + k < count_ref[r], panel, jnp.zeros_like(panel)))
                f = index_ref[r, first + k]
                dz = ((f >> 4) - z) & (NZ - 1)
                dx = ((f >> 2) - x) & (NX - 1)
                block = field[table_ref[dz * NX + dx], f & 3]
                blocks.append(jnp.where(first + k < count_ref[r], block, jnp.zeros_like(block)))
            total[r] += jnp.dot(
                jnp.concatenate(blocks, axis=1),
                jnp.concatenate(sources, axis=0),
                preferred_element_type=jnp.float32,
            )

    for k in range(PANELS):
        if k + LOOKAHEAD < PANELS:
            fetch(k + LOOKAHEAD)
        at, rows = rows_of(k)
        pl.loop(at, at + rows)(contact)

    v = terms[0][...]
    left_at = table_ref[jnp.where(x > 0, 0, NZ - 1) * NX + NX - 1]
    right_at = table_ref[jnp.where(x < NX - 1, 0, 1) * NX + 1]
    left = field[left_at, ROWS - 1][:, BLK - 128 :].astype(jnp.float32)
    right = field[right_at, 0][:, :128].astype(jnp.float32)
    wide = jnp.concatenate([left, v, right], axis=1)
    width = BEADS + 256
    before = pltpu.roll(wide, 1, 1)[:, 128 : 128 + BEADS]
    after = pltpu.roll(wide, width - 1, 1)[:, 128 : 128 + BEADS]
    diagonal, link, prior = (vec_ref[k : k + 1, :] for k in range(3))
    chain = diagonal * v - link * after - prior * before
    contact = jnp.concatenate([total[r] for r in range(ROWS)], axis=1)
    scaled = (chain - contact - CENTER * v) / HALF_WIDTH
    coef = cheb_coef()
    if step == 1:
        new = scaled
    else:
        new = 2.0 * scaled - terms[1][...]
    if step < 3:
        out_ref[...] = new
        put_rounded(new, own_out)
    else:
        out_ref[...] = (
            coef[0] * terms[2][...] + coef[1] * terms[1][...] + coef[2] * v + coef[3] * new
        )


def term_call(step, scalars, pieces, panels, near, vec, terms):
    kept = pltpu.VMEM if step > 1 else pltpu.HBM
    pieces = [pltpu.with_memory_space_constraint(p, kept) for p in pieces]
    panels = [pltpu.with_memory_space_constraint(p, pltpu.HBM) for p in panels]
    near = pltpu.with_memory_space_constraint(near, pltpu.HBM)
    smem = pl.BlockSpec(memory_space=pltpu.SMEM)
    vmem = pl.BlockSpec(memory_space=pltpu.VMEM)
    hbm = pl.BlockSpec(memory_space=pltpu.HBM)
    resident = vmem if step > 1 else hbm
    full = jax.ShapeDtypeStruct((COLS, BEADS), jnp.float32)
    own = jax.ShapeDtypeStruct((ROWS, COLS, BLK), jnp.bfloat16)
    return pl.pallas_call(
        functools.partial(term_kernel, step),
        out_shape=(full, own) if step < 3 else full,
        in_specs=[smem] * 4 + [resident] * len(pieces) + [hbm] * PANELS + [hbm] + [vmem] * (1 + len(terms)),
        out_specs=(vmem,) * 2 if step < 3 else vmem,
        scratch_shapes=[
            pltpu.VMEM((NZ * NX, ROWS, COLS, BLK), jnp.bfloat16),
            pltpu.VMEM((8 * ROWS, CHUNK, BLK, BLK), jnp.bfloat16),
            pltpu.VMEM((ROWS, BLK, BLK), jnp.bfloat16),
            pltpu.VMEM((ROWS, COLS, BLK), jnp.float32),
            pltpu.SemaphoreType.DMA((2,)),
            pltpu.SemaphoreType.DMA((8 * ROWS, CHUNK)),
        ],
        compiler_params=pltpu.CompilerParams(vmem_limit_bytes=VMEM_LIMIT),
        cost_estimate=pl.CostEstimate(
            flops=2 * 128 * COLS * BLK * BLK, bytes_accessed=20 * 2**20, transcendentals=0
        ),
        name=f"term{step}",
    )(*scalars, *pieces, *panels, near, vec, *terms)


def ring_of_panels(own):
    low, high = own[:2], own[2:]
    up_low = take_y(low, 1)
    down_high = take_y(high, -1)
    up_high = take_y(high, 1)
    down_low = take_y(low, -1)
    far_low = take_y(up_low, 1)
    far_high = take_y(down_high, -1)
    return [own, up_low, up_high, down_low, down_high, far_low, far_high]


def per_device(force, pulled, shift, bond, near_panel, far_panel, far_index, far_count):
    genome, group = lax.axis_index("genome"), lax.axis_index("group")
    core = group % NC
    where = jnp.stack([genome // NX, genome % NX, group // NC, core]).astype(jnp.int32)
    offset = lax.iota(jnp.int32, NZ * NX)
    by_place = (where[0] * NX + (offset // NX) * NX) % (NZ * NX) + (where[1] + offset % NX) % NX
    by_pair = jnp.array(pair_tables(), jnp.int32)[core * NX + where[1]]
    first_bead = (genome * BEADS).astype(jnp.int32)

    found = ring_of_panels(far_panel)
    panels = found + [take_core(piece) for piece in found]

    vmem = pl.BlockSpec(memory_space=pltpu.VMEM)
    source, own = pl.pallas_call(
        source_kernel,
        out_shape=(
            jax.ShapeDtypeStruct((COLS, BEADS), jnp.float32),
            jax.ShapeDtypeStruct((ROWS, COLS, BLK), jnp.bfloat16),
        ),
        in_specs=[pl.BlockSpec(memory_space=pltpu.SMEM), vmem, vmem],
        out_specs=(vmem,) * 2,
        name="source",
    )(first_bead[None], pulled[None, :], force)

    position = first_bead + lax.iota(jnp.int32, BEADS)
    link = jnp.where(position < BEADS * NZ * NX - 1, bond, jnp.float32(0.0))
    left_bond = lax.ppermute(link[-1:], "genome", [(g, g + 1) for g in range(NZ * NX - 1)])
    prior = jnp.concatenate([left_bond, link[:-1]])
    vec = jnp.stack([shift + link + prior, link, prior])

    everyone = lax.all_gather(own, "genome")
    scalars = (where, by_place, far_index, far_count)
    one, own = term_call(1, scalars, [everyone], panels, near_panel, vec, [source])
    scalars = (where, by_pair, far_index, far_count)
    two, own = term_call(2, scalars, gathered(own), panels, near_panel, vec, [one, source])
    return term_call(3, scalars, gathered(own), panels, near_panel, vec, [two, one, source])


def solution(mesh):
    in_specs = (
        P("group", "genome"),
        P("group"),
        P("genome"),
        P("genome"),
        P("genome", None, None),
        P("genome", "group", None, None),
        P("genome", None),
        P("genome"),
    )
    out_specs = P("group", "genome")
    return jax.shard_map(
        per_device, mesh=mesh, in_specs=in_specs, out_specs=out_specs, check_vma=False
    )
```
